32 devices in a mesh: groups: 2 (over x), blk: 8 (over z, y), split: 2 (over core).
Axes of the slice: x: 2, y: 2, z: 4, core: 2. Of those that a mesh axis runs over, the one named last changes fastest.
Arguments:
- tiles: bfloat16 [8192, 1536], P(('groups', 'blk')), parts along dimension 0, may hold values from -6 to 6
- landmarks: bfloat16 [2048, 1536], P(('blk', 'split')), may hold values from -6 to 6
- projection: bfloat16 [2048, 1024], P(('blk', 'split')), may hold values from -0.125 to 0.125
- offsets: float32 [2048], P(('blk', 'split')), may hold values from 0 to 2
Outputs:
- coords: bfloat16 [8192, 1024], P(('groups', 'blk')), parts along dimension 0
- energy: float32 [8192], P(('groups', 'blk')), parts along dimension 0
The draws below stay inside these ranges and needn't reach their ends.
There are 2 independent parts, one for each index of `groups`. The reference program is written for one: setup_inputs(seed, part) draws one part's arguments, and reference() takes and returns one part's arrays. A program takes and returns all parts, laid end to end along the dimension named above; an argument that names none is the same for every part. Nothing has to cross between parts.
All inputs are finite; a program needn't handle non-finite values.
Results may differ from the reference program's by a relative error of at most 0.012.
Values may be sent and summed in bfloat16 or wider, within the bound.
A program may use at most 64 MiB of HBM per device.

```python
import jax
import jax.numpy as jnp
from jax import lax

E = 1536
K = 1024
LM_DEV = 128
TILES = 4096
LM = 2048


def block_scale(own_key, dims, pieces, low, top_value):
    gain, own = 1.0, jax.random.fold_in(own_key, 6)
    for axis_at, shards_of in pieces:
        draws = jnp.exp(jax.random.uniform(jax.random.fold_in(own, axis_at), (shards_of,), jnp.float32, low / len(pieces), top_value / len(pieces)))
        gain = gain * jnp.repeat(draws, dims[axis_at] // shards_of).reshape([-1 if axis == axis_at else 1 for axis in range(len(dims))])
    return gain


def scatter_about(stream_key, shape, width, limit, pieces=(), kind=jnp.bfloat16):
    result = jax.random.normal(stream_key, shape, jnp.float32) * width
    if len(pieces) > 0:
        result = block_scale(stream_key, shape, pieces, -0.22, 0.18) * result
    return jnp.clip(result, min=-limit, max=limit).astype(kind)


def setup_inputs(seed: int = 0, part: int = 0) -> dict:
    arg_keys = jax.random.split(jax.random.key(seed), 5)
    part_keys = jax.random.split(jax.random.fold_in(arg_keys[4], part), 5)
    tiles = scatter_about(part_keys[0], (TILES, E), 1.0, 6.0, ((0, 8),))
    landmarks = scatter_about(arg_keys[1], (LM, E), 1.0, 6.0, ((0, 16),))
    projection = scatter_about(arg_keys[2], (LM, K), LM ** -0.5, 0.125, ((0, 16),))
    offsets = jnp.clip(2.0 * jax.random.uniform(arg_keys[3], (LM,), jnp.float32) ** block_scale(arg_keys[3], (LM,), ((0, 16),), -0.2, 0.2), 0.0, 2.0)
    return {"tiles": tiles, "landmarks": landmarks, "projection": projection, "offsets": offsets}


def reference(tiles, landmarks, projection, offsets):
    scale = 1.0 / (E ** 0.5)
    blocks = LM // LM_DEV
    land_blocks = landmarks.reshape(blocks, LM_DEV, E)
    proj_blocks = projection.reshape(blocks, LM_DEV, K)
    off_blocks = offsets.reshape(blocks, LM_DEV)

    def step(total, items):
        land, proj, off = items
        scores = lax.dot_general(tiles, land, (((1,), (1,)), ((), ())), preferred_element_type=jnp.float32)
        kernel = jnp.exp(scores * scale - off[None, :]).astype(jnp.bfloat16)
        return total + jnp.dot(kernel, proj, preferred_element_type=jnp.float32), None

    start = jnp.zeros((tiles.shape[0], K), jnp.float32)
    coords_full, unused = lax.scan(step, start, (land_blocks, proj_blocks, off_blocks))
    energy = jnp.log(jnp.mean(coords_full * coords_full, axis=1) + 1e-6)
    return coords_full.astype(jnp.bfloat16), energy
```

```python
import functools

import jax
import jax.numpy as jnp
from jax import lax
from jax.experimental import pallas as pl
from jax.experimental.pallas import tpu as pltpu
from jax.sharding import PartitionSpec as P

MESH = pl.DeviceIdType.MESH
UP, DOWN, ACROSS, SIB = 0, 1, 2, 3


def kernel(
    nb, ny, chunks,
    tiles, land, proj, off, out, energy,
    t_buf, l_buf, o_buf, p_buf, k_buf, acc, x_out, x_in, c_buf, e_buf, sq,
    r_land, r_off, r_proj, s_land, s_off, s_proj,
    loc_sem, t_send, t_recv, xs_sem, xr_sem, c_send, c_recv, c_loc, e_sem,
):
    nz = nb // ny
    g, me, s = lax.axis_index("groups"), lax.axis_index("blk"), lax.axis_index("split")
    half = lax.rem(g, 2)
    z, y = me // ny, lax.rem(me, ny)
    rows_t = t_buf.shape[0] // 2
    hr = l_buf.shape[2]
    width_k = acc.shape[1]
    kc = width_k // chunks
    scale = 1.0 / l_buf.shape[3] ** 0.5

    mate = {"groups": g + 1 - 2 * half}
    sib = {"split": 1 - s}
    peers = {
        UP: ({"blk": me + ny}, z + 1 < nz),
        DOWN: ({"blk": me - ny}, z > 0),
        ACROSS: ({"blk": me + 1 - 2 * y}, None),
        SIB: (sib, None),
    }
    dirs = [UP, DOWN, SIB] + ([ACROSS] if ny == 2 else [])

    def guard(cond, fn):
        if cond is None:
            fn()
        else:
            pl.when(cond)(fn)

    barrier = pltpu.get_barrier_semaphore()

    def greet(dev):
        pl.semaphore_signal(barrier, inc=1, device_id=dev, device_id_type=MESH)

    greet(mate)
    for d in dirs:
        guard(peers[d][1], functools.partial(greet, peers[d][0]))
    pl.semaphore_wait(
        barrier,
        len(dirs) - 1 + (z + 1 < nz).astype(jnp.int32) + (z > 0).astype(jnp.int32),
    )

    def rc(src, dst, ss, rs, dev):
        return pltpu.make_async_remote_copy(
            src_ref=src, dst_ref=dst, send_sem=ss, recv_sem=rs, device_id=dev, device_id_type=MESH
        )

    sent = []

    def begin(src, dst, ss, rs, dev, cond):
        guard(cond, lambda: rc(src, dst, ss, rs, dev).start())
        sent.append((src, dst, ss, rs, dev, cond))

    def both(a, b):
        if a is None:
            return b
        return a if b is None else jnp.logical_and(a, b)

    def pieces(kind, b, t):
        if kind == "land":
            return [(o_buf.at[b, t], r_off.at[b, t], s_off), (l_buf.at[b, t], r_land.at[b, t], s_land)]
        return [(p_buf.at[kind, b, t], r_proj.at[kind, b, t], s_proj.at[kind])]

    def own_src(kind):
        mine = pl.ds(half * hr, hr)
        if kind == "land":
            return [off.at[half], land.at[mine, :]]
        return [proj.at[mine, pl.ds(kind * kc, kc)]]

    def send(kind, b, d, cond=None, own=False):
        dev, exists = peers[d]
        for i, (ref, rs, ss) in enumerate(pieces(kind, b, s)):
            src = own_src(kind)[i] if own else ref
            begin(src, ref, ss.at[d, b], rs, dev, both(cond, exists))

    def await_piece(kind, b, t, cond=None):
        def go():
            for ref, rs, ss in pieces(kind, b, t):
                rc(ref, ref, rs, rs, sib).wait_recv()
        guard(cond, go)

    def send_own(kind):
        for d in dirs:
            send(kind, me, d, own=True)

    def across_of(b):
        return b + 1 - 2 * lax.rem(b, 2)

    def relay(kind, k):
        if k == 0:
            cands = [(me, None, None)]
        else:
            cands = [(me - ny * k, z - k >= 0, UP), (me + ny * k, z + k < nz, DOWN)]
        for b, cond, d in cands:
            if d is not None:
                b = jnp.where(cond, b, me)
                await_piece(kind, b, s, cond)
                send(kind, b, d, cond)
                if ny == 2:
                    send(kind, b, ACROSS, cond)
                send(kind, b, SIB, cond)
        if ny == 2:
            for b, cond, d in cands:
                if d is not None:
                    b = jnp.where(cond, b, me)
                await_piece(kind, across_of(b), s, cond)
                send(kind, across_of(b), SIB, cond)

    my_rows = tiles.at[pl.ds(s * rows_t, rows_t), :]
    begin(my_rows, t_buf.at[pl.ds(rows_t, rows_t), :], t_send, t_recv, mate, None)
    send_own("land")
    own_tiles = pltpu.make_async_copy(my_rows, t_buf.at[pl.ds(0, rows_t), :], loc_sem.at[0])
    own_tiles.start()
    own_off = pltpu.make_async_copy(off.at[half], o_buf.at[me, s], loc_sem.at[1])
    own_off.start()
    own_land = pltpu.make_async_copy(own_src("land")[1], l_buf.at[me, s], loc_sem.at[2])
    own_land.start()
    own_proj = []
    for c in range(chunks):
        cp = pltpu.make_async_copy(own_src(c)[0], p_buf.at[c, me, s], loc_sem.at[3 + c])
        cp.start()
        own_proj.append(cp)

    for k in range(nz):
        relay("land", k)
    for c in range(chunks):
        send_own(c)

    own_tiles.wait()
    own_off.wait()
    own_land.wait()

    def others(kind):
        def body(b, carry):
            await_piece(kind, b, 1 - s)
            return carry
        lax.fori_loop(0, nb, body, 0)

    others("land")
    group = 2 if nb % 2 == 0 else 1
    gw = group * 2 * hr

    def scores(row0):
        def body(i, carry):
            rhs = l_buf[pl.ds(i * group, group)].reshape(gw, l_buf.shape[3])
            sc = lax.dot_general(
                t_buf[pl.ds(row0, rows_t), :], rhs, (((1,), (1,)), ((), ())),
                preferred_element_type=jnp.float32,
            )
            ob = o_buf[pl.ds(i * group, group)]
            ob = (ob[:, 0] + ob[:, 1])
            ob = jnp.concatenate([ob[j] for j in range(group)], axis=1)
            k_buf[i, pl.ds(row0, rows_t), :] = jnp.exp(sc * scale - ob).astype(jnp.bfloat16)
            return carry
        lax.fori_loop(0, nb // group, body, 0)

    scores(0)
    rc(my_rows, t_buf.at[pl.ds(rows_t, rows_t), :], t_send, t_recv, mate).wait_recv()
    scores(rows_t)

    def project(c, row0):
        total = jnp.zeros((rows_t, kc), jnp.float32)
        def body(i, total):
            rhs = p_buf[c, pl.ds(i * group, group)].reshape(gw, kc)
            return total + jnp.dot(
                k_buf[i, pl.ds(row0, rows_t), :], rhs, preferred_element_type=jnp.float32
            )
        return lax.fori_loop(0, nb // group, body, total, unroll=nb <= 8)

    def finish(c):
        rc(x_in.at[c], x_in.at[c], xs_sem.at[c], xr_sem.at[c], mate).wait_recv()
        cols = pl.ds(c * kc, kc)
        full = acc[:, cols] + x_in[c].astype(jnp.float32)
        c_buf[c] = full.astype(jnp.bfloat16)
        where = out.at[pl.ds(s * rows_t, rows_t), cols]
        begin(c_buf.at[c], where, c_send.at[c], c_recv.at[c], sib, None)
        pltpu.make_async_copy(c_buf.at[c], where, c_loc.at[c]).start()
        squares = full * full
        part = squares[:, 0:128]
        for j in range(1, kc // 128):
            part = part + squares[:, j * 128:(j + 1) * 128]
        sq[...] = part if c == 0 else sq[...] + part

    for c in range(chunks):
        for k in range(nz):
            relay(c, k)
        own_proj[c].wait()
        others(c)
        x_out[c] = project(c, rows_t).astype(jnp.bfloat16)
        begin(x_out.at[c], x_in.at[c], xs_sem.at[c], xr_sem.at[c], mate, None)
        acc[:, pl.ds(c * kc, kc)] = project(c, 0)
        if c > 0:
            finish(c - 1)
    finish(chunks - 1)

    total = jnp.sum(sq[...].T, axis=0, keepdims=True)
    e_buf[...] = jnp.log(total / width_k + 1e-6)
    begin(e_buf, energy.at[s], e_sem.at[0], e_sem.at[1], sib, None)
    e_loc = pltpu.make_async_copy(e_buf, energy.at[s], e_sem.at[2])
    e_loc.start()
    e_loc.wait()
    for c in range(chunks):
        cols = pl.ds(c * kc, kc)
        mine = out.at[pl.ds(s * rows_t, rows_t), cols]
        pltpu.make_async_copy(c_buf.at[c], mine, c_loc.at[c]).wait()
        theirs = out.at[pl.ds((1 - s) * rows_t, rows_t), cols]
        rc(c_buf.at[c], theirs, c_send.at[c], c_recv.at[c], sib).wait_recv()
    rc(e_buf, energy.at[1 - s], e_sem.at[0], e_sem.at[1], sib).wait_recv()
    for src, dst, ss, rs, dev, cond in sent:
        guard(cond, lambda: rc(src, dst, ss, rs, dev).wait_send())


def solution(mesh):
    nb = mesh.shape["blk"]
    ny = 2 if nb % 2 == 0 and nb <= 8 else 1

    def per_device(tiles, landmarks, projection, offsets):
        rows, width = tiles.shape
        hr, rows_t = landmarks.shape[0] // 2, rows // 2
        width_k = projection.shape[1]
        chunks = 4
        kc = width_k // chunks
        s = lax.axis_index("split")
        at = lax.broadcasted_iota(jnp.int32, (2, 2, hr), 1) == s
        off = jnp.where(at, offsets.reshape(2, 1, hr), 0.0).reshape(2, 1, 2 * hr)
        group = 2 if nb % 2 == 0 else 1
        bf, f32 = jnp.bfloat16, jnp.float32
        dma = pltpu.SemaphoreType.DMA
        coords, energy = pl.pallas_call(
            functools.partial(kernel, nb, ny, chunks),
            out_shape=(
                jax.ShapeDtypeStruct((rows, width_k), bf),
                jax.ShapeDtypeStruct((2, 1, rows_t), f32),
            ),
            in_specs=[pl.BlockSpec(memory_space=pl.ANY)] * 4,
            out_specs=[pl.BlockSpec(memory_space=pl.ANY)] * 2,
            scratch_shapes=[
                pltpu.VMEM((rows, width), bf),
                pltpu.VMEM((nb, 2, hr, width), bf),
                pltpu.VMEM((nb, 2, 1, 2 * hr), f32),
                pltpu.VMEM((chunks, nb, 2, hr, kc), bf),
                pltpu.VMEM((nb // group, rows, group * 2 * hr), bf),
                pltpu.VMEM((rows_t, width_k), f32),
                pltpu.VMEM((chunks, rows_t, kc), bf),
                pltpu.VMEM((chunks, rows_t, kc), bf),
                pltpu.VMEM((chunks, rows_t, kc), bf),
                pltpu.VMEM((1, rows_t), f32),
                pltpu.VMEM((rows_t, 128), f32),
                dma((nb, 2)), dma((nb, 2)), dma((chunks, nb, 2)),
                dma((4, nb)), dma((4, nb)), dma((chunks, 4, nb)),
                dma((3 + chunks,)), dma, dma, dma((chunks,)), dma((chunks,)),
                dma((chunks,)), dma((chunks,)), dma((chunks,)), dma((3,)),
            ],
            compiler_params=pltpu.CompilerParams(
                collective_id=0, has_side_effects=True, vmem_limit_bytes=56 * 2**20
            ),
        )(tiles, landmarks, projection, off)
        return coords, energy.reshape(rows)

    return jax.shard_map(
        per_device,
        mesh=mesh,
        in_specs=(
            P(("groups", "blk"), None),
            P(("blk", "split"), None),
            P(("blk", "split"), None),
            P(("blk", "split")),
        ),
        out_specs=(P(("groups", "blk"), None), P(("groups", "blk"))),
        check_vma=False,
    )
```

```python
import functools

import jax
import jax.numpy as jnp
from jax import lax
from jax.experimental import pallas as pl
from jax.experimental.pallas import tpu as pltpu
from jax.sharding import PartitionSpec as P

MESH = pl.DeviceIdType.MESH
UP, DOWN, ACROSS, SIB = 0, 1, 2, 3


def kernel(
    nb, ny, chunks,
    tiles, land, proj, off, out, energy,
    t_buf, l_buf, o_buf, p_buf, k_buf, acc, x_out, x_in, c_buf, e_buf, sq,
    r_land, r_off, r_proj, s_land, s_off, s_proj,
    loc_sem, t_send, t_recv, xs_sem, xr_sem, c_send, c_recv, c_loc, e_sem,
):
    nz = nb // ny
    g, me, s = lax.axis_index("groups"), lax.axis_index("blk"), lax.axis_index("split")
    half = lax.rem(g, 2)
    z, y = me // ny, lax.rem(me, ny)
    rows_t = t_buf.shape[0] // 2
    hr = l_buf.shape[2]
    width_k = acc.shape[1]
    kc = width_k // chunks
    lp = r_land.shape[0]
    pr = hr // lp
    J = lp + chunks
    lead = 2
    scale = 1.0 / l_buf.shape[3] ** 0.5

    mate = {"groups": g + 1 - 2 * half}
    sib = {"split": 1 - s}
    peers = {
        UP: ({"blk": me + ny}, z + 1 < nz),
        DOWN: ({"blk": me - ny}, z > 0),
        ACROSS: ({"blk": me + 1 - 2 * y}, None),
        SIB: (sib, None),
    }
    dirs = [UP, DOWN, SIB] + ([ACROSS] if ny == 2 else [])

    def guard(cond, fn):
        if cond is None:
            fn()
        else:
            pl.when(cond)(fn)

    barrier = pltpu.get_barrier_semaphore()

    def greet(dev):
        pl.semaphore_signal(barrier, inc=1, device_id=dev, device_id_type=MESH)

    greet(mate)
    for d in dirs:
        guard(peers[d][1], functools.partial(greet, peers[d][0]))
    pl.semaphore_wait(
        barrier,
        len(dirs) - 1 + (z + 1 < nz).astype(jnp.int32) + (z > 0).astype(jnp.int32),
    )

    def rc(src, dst, ss, rs, dev):
        return pltpu.make_async_remote_copy(
            src_ref=src, dst_ref=dst, send_sem=ss, recv_sem=rs, device_id=dev, device_id_type=MESH
        )

    sent = []

    def begin(src, dst, ss, rs, dev, cond):
        guard(cond, lambda: rc(src, dst, ss, rs, dev).start())
        sent.append((src, dst, ss, rs, dev, cond))

    def both(a, b):
        if a is None:
            return b
        return a if b is None else jnp.logical_and(a, b)

    def pieces(j, b, t):
        if j >= lp:
            c = j - lp
            return [(p_buf.at[c, b, t], r_proj.at[c, b, t], s_proj.at[c])]
        out = [(l_buf.at[b, t, pl.ds(j * pr, pr), :], r_land.at[j, b, t], s_land.at[j])]
        if j == 0:
            out.append((o_buf.at[b, t], r_off.at[b, t], s_off))
        return out

    def own_src(j):
        if j >= lp:
            return [proj.at[pl.ds(half * hr, hr), pl.ds((j - lp) * kc, kc)]]
        out = [land.at[pl.ds(half * hr + j * pr, pr), :]]
        if j == 0:
            out.append(off.at[half])
        return out

    def send(kind, b, d, cond=None, own=False):
        dev, exists = peers[d]
        for i, (ref, rs, ss) in enumerate(pieces(kind, b, s)):
            src = own_src(kind)[i] if own else ref
            begin(src, ref, ss.at[d, b], rs, dev, both(cond, exists))

    def await_piece(kind, b, t, cond=None):
        def go():
            for ref, rs, ss in pieces(kind, b, t):
                rc(ref, ref, rs, rs, sib).wait_recv()
        guard(cond, go)

    def send_own(kind):
        for d in dirs:
            send(kind, me, d, own=True)

    def across_of(b):
        return b + 1 - 2 * lax.rem(b, 2)

    def cands(k):
        return [(me - ny * k, z - k >= 0, UP), (me + ny * k, z + k < nz, DOWN)]

    def relay(j, k):
        for b, cond, d in cands(k):
            b = jnp.where(cond, b, me)
            await_piece(j, b, s, cond)
            send(j, b, d, cond)
            if ny == 2:
                send(j, b, ACROSS, cond)
            send(j, b, SIB, cond)

    def arrive_across(j, k):
        for b, cond, d in ([(me, None, None)] if k == 0 else cands(k)):
            if d is not None:
                b = jnp.where(cond, b, me)
            await_piece(j, across_of(b), s, cond)
            send(j, across_of(b), SIB, cond)

    def step(t):
        if t < J and t >= lead:
            send_own(t)
        for k in range(1, nz):
            if 0 <= t - k < J:
                relay(t - k, k)
        if ny == 2:
            for k in range(nz):
                if 0 <= t - 1 - k < J:
                    arrive_across(t - 1 - k, k)

    my_rows = tiles.at[pl.ds(s * rows_t, rows_t), :]
    begin(my_rows, t_buf.at[pl.ds(rows_t, rows_t), :], t_send, t_recv, mate, None)
    for j in range(lead):
        send_own(j)
    own_tiles = pltpu.make_async_copy(my_rows, t_buf.at[pl.ds(0, rows_t), :], loc_sem.at[0])
    own_tiles.start()
    own_off = pltpu.make_async_copy(off.at[half], o_buf.at[me, s], loc_sem.at[1])
    own_off.start()
    own_land = pltpu.make_async_copy(land.at[pl.ds(half * hr, hr), :], l_buf.at[me, s], loc_sem.at[2])
    own_land.start()
    own_proj = []
    for c in range(chunks):
        cp = pltpu.make_async_copy(own_src(lp + c)[0], p_buf.at[c, me, s], loc_sem.at[3 + c])
        cp.start()
        own_proj.append(cp)

    last = nz - 1 + (1 if ny == 2 else 0)
    for t in range(lp + last):
        step(t)
    step(lp + last)

    own_tiles.wait()
    own_off.wait()
    own_land.wait()

    def others(kind):
        def body(b, carry):
            await_piece(kind, b, 1 - s)
            return carry
        lax.fori_loop(0, nb, body, 0)

    for j in range(lp):
        others(j)
    group = 2 if nb % 2 == 0 else 1
    gw = group * 2 * hr

    def scores(row0):
        def body(i, carry):
            rhs = l_buf[pl.ds(i * group, group)].reshape(gw, l_buf.shape[3])
            sc = lax.dot_general(
                t_buf[pl.ds(row0, rows_t), :], rhs, (((1,), (1,)), ((), ())),
                preferred_element_type=jnp.float32,
            )
            ob = o_buf[pl.ds(i * group, group)]
            ob = jnp.concatenate([ob[j, t] for j in range(group) for t in range(2)], axis=1)
            k_buf[i, pl.ds(row0, rows_t), :] = jnp.exp(sc * scale - ob).astype(jnp.bfloat16)
            return carry
        lax.fori_loop(0, nb // group, body, 0)

    scores(0)
    rc(my_rows, t_buf.at[pl.ds(rows_t, rows_t), :], t_send, t_recv, mate).wait_recv()
    scores(rows_t)

    def project(c, row0):
        total = jnp.zeros((rows_t, kc), jnp.float32)
        def body(i, total):
            rhs = p_buf[c, pl.ds(i * group, group)].reshape(gw, kc)
            return total + jnp.dot(
                k_buf[i, pl.ds(row0, rows_t), :], rhs, preferred_element_type=jnp.float32
            )
        return lax.fori_loop(0, nb // group, body, total, unroll=nb <= 8)

    def finish(c):
        rc(x_in.at[c], x_in.at[c], xs_sem.at[c], xr_sem.at[c], mate).wait_recv()
        cols = pl.ds(c * kc, kc)
        full = acc[:, cols] + x_in[c].astype(jnp.float32)
        c_buf[c] = full.astype(jnp.bfloat16)
        where = out.at[pl.ds(s * rows_t, rows_t), cols]
        begin(c_buf.at[c], where, c_send.at[c], c_recv.at[c], sib, None)
        pltpu.make_async_copy(c_buf.at[c], where, c_loc.at[c]).start()
        squares = full * full
        part = squares[:, 0:128]
        for j in range(1, kc // 128):
            part = part + squares[:, j * 128:(j + 1) * 128]
        sq[...] = part if c == 0 else sq[...] + part

    for c in range(chunks):
        step(lp + last + c + 1)
        own_proj[c].wait()
        others(lp + c)
        x_out[c] = project(c, rows_t).astype(jnp.bfloat16)
        begin(x_out.at[c], x_in.at[c], xs_sem.at[c], xr_sem.at[c], mate, None)
        acc[:, pl.ds(c * kc, kc)] = project(c, 0)
        if c > 0:
            finish(c - 1)
    finish(chunks - 1)

    total = jnp.sum(sq[...].T, axis=0, keepdims=True)
    e_buf[...] = jnp.log(total / width_k + 1e-6)
    begin(e_buf, energy.at[s], e_sem.at[0], e_sem.at[1], sib, None)
    e_loc = pltpu.make_async_copy(e_buf, energy.at[s], e_sem.at[2])
    e_loc.start()
    e_loc.wait()
    for c in range(chunks):
        cols = pl.ds(c * kc, kc)
        mine = out.at[pl.ds(s * rows_t, rows_t), cols]
        pltpu.make_async_copy(c_buf.at[c], mine, c_loc.at[c]).wait()
        theirs = out.at[pl.ds((1 - s) * rows_t, rows_t), cols]
        rc(c_buf.at[c], theirs, c_send.at[c], c_recv.at[c], sib).wait_recv()
    rc(e_buf, energy.at[1 - s], e_sem.at[0], e_sem.at[1], sib).wait_recv()
    for src, dst, ss, rs, dev, cond in sent:
        guard(cond, lambda: rc(src, dst, ss, rs, dev).wait_send())


def solution(mesh):
    nb = mesh.shape["blk"]
    ny = 2 if nb % 2 == 0 and nb <= 8 else 1

    def per_device(tiles, landmarks, projection, offsets):
        rows, width = tiles.shape
        hr, rows_t = landmarks.shape[0] // 2, rows // 2
        width_k = projection.shape[1]
        chunks = 4
        kc = width_k // chunks
        lp = 4 if hr % 64 == 0 and nb <= 8 else 1
        off = offsets.reshape(2, 1, hr)
        group = 2 if nb % 2 == 0 else 1
        bf, f32 = jnp.bfloat16, jnp.float32
        dma = pltpu.SemaphoreType.DMA
        coords, energy = pl.pallas_call(
            functools.partial(kernel, nb, ny, chunks),
            out_shape=(
                jax.ShapeDtypeStruct((rows, width_k), bf),
                jax.ShapeDtypeStruct((2, 1, rows_t), f32),
            ),
            in_specs=[pl.BlockSpec(memory_space=pl.ANY)] * 4,
            out_specs=[pl.BlockSpec(memory_space=pl.ANY)] * 2,
            scratch_shapes=[
                pltpu.VMEM((rows, width), bf),
                pltpu.VMEM((nb, 2, hr, width), bf),
                pltpu.VMEM((nb, 2, 1, hr), f32),
                pltpu.VMEM((chunks, nb, 2, hr, kc), bf),
                pltpu.VMEM((nb // group, rows, group * 2 * hr), bf),
                pltpu.VMEM((rows_t, width_k), f32),
                pltpu.VMEM((chunks, rows_t, kc), bf),
                pltpu.VMEM((chunks, rows_t, kc), bf),
                pltpu.VMEM((chunks, rows_t, kc), bf),
                pltpu.VMEM((1, rows_t), f32),
                pltpu.VMEM((rows_t, 128), f32),
                dma((lp, nb, 2)), dma((nb, 2)), dma((chunks, nb, 2)),
                dma((lp, 4, nb)), dma((4, nb)), dma((chunks, 4, nb)),
                dma((3 + chunks,)), dma, dma, dma((chunks,)), dma((chunks,)),
                dma((chunks,)), dma((chunks,)), dma((chunks,)), dma((3,)),
            ],
            compiler_params=pltpu.CompilerParams(
                collective_id=0, has_side_effects=True, vmem_limit_bytes=56 * 2**20
            ),
        )(tiles, landmarks, projection, off)
        return coords, energy.reshape(rows)

    return jax.shard_map(
        per_device,
        mesh=mesh,
        in_specs=(
            P(("groups", "blk"), None),
            P(("blk", "split"), None),
            P(("blk", "split"), None),
            P(("blk", "split")),
        ),
        out_specs=(P(("groups", "blk"), None), P(("groups", "blk"))),
        check_vma=False,
    )
```

```python
import functools

import jax
import jax.numpy as jnp
from jax import lax
from jax.experimental import pallas as pl
from jax.experimental.pallas import tpu as pltpu
from jax.sharding import PartitionSpec as P

MESH = pl.DeviceIdType.MESH
UP, DOWN, ACROSS, SIB = 0, 1, 2, 3


def kernel(
    nb, ny, chunks,
    tiles, land, proj, off, out, energy,
    t_buf, l_buf, o_buf, p_buf, k_buf, acc, x_out, x_in, c_buf, e_buf, sq,
    r_land, r_off, r_proj, s_land, s_off, s_proj,
    loc_sem, t_send, t_recv, xs_sem, xr_sem, c_send, c_recv, c_loc, e_sem,
):
    nz = nb // ny
    g, me, s = lax.axis_index("groups"), lax.axis_index("blk"), lax.axis_index("split")
    half = lax.rem(g, 2)
    z, y = me // ny, lax.rem(me, ny)
    rows_t = t_buf.shape[0] // 2
    hr = l_buf.shape[2]
    width_k = acc.shape[1]
    kc = width_k // chunks
    lp = r_land.shape[0]
    pr = hr // lp
    J = lp + chunks
    lead = 2
    turned = (lp, lp + 2) if ny == 2 else ()
    scale = 1.0 / l_buf.shape[3] ** 0.5

    mate = {"groups": g + 1 - 2 * half}
    sib = {"split": 1 - s}
    peers = {
        UP: ({"blk": me + ny}, z + 1 < nz),
        DOWN: ({"blk": me - ny}, z > 0),
        ACROSS: ({"blk": me + 1 - 2 * y}, None),
        SIB: (sib, None),
    }
    dirs = [UP, DOWN, SIB] + ([ACROSS] if ny == 2 else [])

    def guard(cond, fn):
        if cond is None:
            fn()
        else:
            pl.when(cond)(fn)

    barrier = pltpu.get_barrier_semaphore()

    def greet(dev):
        pl.semaphore_signal(barrier, inc=1, device_id=dev, device_id_type=MESH)

    greet(mate)
    for d in dirs:
        guard(peers[d][1], functools.partial(greet, peers[d][0]))
    pl.semaphore_wait(
        barrier,
        len(dirs) - 1 + (z + 1 < nz).astype(jnp.int32) + (z > 0).astype(jnp.int32),
    )

    def rc(src, dst, ss, rs, dev):
        return pltpu.make_async_remote_copy(
            src_ref=src, dst_ref=dst, send_sem=ss, recv_sem=rs, device_id=dev, device_id_type=MESH
        )

    sent = []

    def begin(src, dst, ss, rs, dev, cond):
        guard(cond, lambda: rc(src, dst, ss, rs, dev).start())
        sent.append((src, dst, ss, rs, dev, cond))

    def both(a, b):
        if a is None:
            return b
        return a if b is None else jnp.logical_and(a, b)

    def pieces(j, b, t):
        if j >= lp:
            c = j - lp
            return [(p_buf.at[c, b, t], r_proj.at[c, b, t], s_proj.at[c])]
        out = [(l_buf.at[b, t, pl.ds(j * pr, pr), :], r_land.at[j, b, t], s_land.at[j])]
        if j == 0:
            out.append((o_buf.at[b, t], r_off.at[b, t], s_off))
        return out

    def own_src(j):
        if j >= lp:
            return [proj.at[pl.ds(half * hr, hr), pl.ds((j - lp) * kc, kc)]]
        out = [land.at[pl.ds(half * hr + j * pr, pr), :]]
        if j == 0:
            out.append(off.at[half])
        return out

    def send(kind, b, d, cond=None, own=False):
        dev, exists = peers[d]
        for i, (ref, rs, ss) in enumerate(pieces(kind, b, s)):
            src = own_src(kind)[i] if own else ref
            begin(src, ref, ss.at[d, b], rs, dev, both(cond, exists))

    def await_piece(kind, b, t, cond=None):
        def go():
            for ref, rs, ss in pieces(kind, b, t):
                rc(ref, ref, rs, rs, sib).wait_recv()
        guard(cond, go)

    def send_own(kind):
        for d in dirs:
            send(kind, me, d, own=True)

    def across_of(b):
        return b + 1 - 2 * lax.rem(b, 2)

    def cands(k):
        return [(me - ny * k, z - k >= 0, UP), (me + ny * k, z + k < nz, DOWN)]

    def relay(j, k):
        for b, cond, d in cands(k):
            b = jnp.where(cond, b, me)
            await_piece(j, b, s, cond)
            send(j, b, d, cond)
            if ny == 2 and j not in turned:
                send(j, b, ACROSS, cond)
            send(j, b, SIB, cond)

    def arrive_across(j, k):
        for b, cond, d in ([(me, None, None)] if k == 0 else cands(k)):
            if d is not None:
                b = jnp.where(cond, b, me)
            b = across_of(b)
            await_piece(j, b, s, cond)
            if j in turned:
                for way in ([UP, DOWN] if d is None else [d]):
                    send(j, b, way, cond)
            send(j, b, SIB, cond)

    def relays(t):
        if t < J and t >= lead:
            send_own(t)
        for k in range(1, nz):
            if 0 <= t - k < J:
                relay(t - k, k)

    def crossings(t):
        if ny == 2:
            for k in range(nz):
                if 0 <= t - 1 - k < J:
                    arrive_across(t - 1 - k, k)

    my_rows = tiles.at[pl.ds(s * rows_t, rows_t), :]
    begin(my_rows, t_buf.at[pl.ds(rows_t, rows_t), :], t_send, t_recv, mate, None)
    for j in range(lead):
        send_own(j)
    own_tiles = pltpu.make_async_copy(my_rows, t_buf.at[pl.ds(0, rows_t), :], loc_sem.at[0])
    own_tiles.start()
    own_off = pltpu.make_async_copy(off.at[half], o_buf.at[me, s], loc_sem.at[1])
    own_off.start()
    own_land = pltpu.make_async_copy(land.at[pl.ds(half * hr, hr), :], l_buf.at[me, s], loc_sem.at[2])
    own_land.start()
    own_proj = []
    for c in range(chunks):
        cp = pltpu.make_async_copy(own_src(lp + c)[0], p_buf.at[c, me, s], loc_sem.at[3 + c])
        cp.start()
        own_proj.append(cp)

    last = nz - 1 + (1 if ny == 2 else 0)
    for t in range(lp + last):
        relays(t)
        crossings(t)
    relays(lp + last)

    own_tiles.wait()
    own_off.wait()
    own_land.wait()

    def others(kind):
        def body(b, carry):
            await_piece(kind, b, 1 - s)
            return carry
        lax.fori_loop(0, nb, body, 0)

    for j in range(lp):
        others(j)
    group = 2 if nb % 2 == 0 else 1
    gw = group * 2 * hr

    def scores(row0):
        def body(i, carry):
            rhs = l_buf[pl.ds(i * group, group)].reshape(gw, l_buf.shape[3])
            sc = lax.dot_general(
                t_buf[pl.ds(row0, rows_t), :], rhs, (((1,), (1,)), ((), ())),
                preferred_element_type=jnp.float32,
            )
            ob = o_buf[pl.ds(i * group, group)]
            ob = jnp.concatenate([ob[j, t] for j in range(group) for t in range(2)], axis=1)
            k_buf[i, pl.ds(row0, rows_t), :] = jnp.exp(sc * scale - ob).astype(jnp.bfloat16)
            return carry
        lax.fori_loop(0, nb // group, body, 0)

    scores(0)
    rc(my_rows, t_buf.at[pl.ds(rows_t, rows_t), :], t_send, t_recv, mate).wait_recv()
    scores(rows_t)

    def project(c, row0):
        total = jnp.zeros((rows_t, kc), jnp.float32)
        def body(i, total):
            rhs = p_buf[c, pl.ds(i * group, group)].reshape(gw, kc)
            return total + jnp.dot(
                k_buf[i, pl.ds(row0, rows_t), :], rhs, preferred_element_type=jnp.float32
            )
        return lax.fori_loop(0, nb // group, body, total, unroll=nb <= 8)

    def finish(c):
        rc(x_in.at[c], x_in.at[c], xs_sem.at[c], xr_sem.at[c], mate).wait_recv()
        cols = pl.ds(c * kc, kc)
        full = acc[:, cols] + x_in[c].astype(jnp.float32)
        c_buf[c] = full.astype(jnp.bfloat16)
        where = out.at[pl.ds(s * rows_t, rows_t), cols]
        begin(c_buf.at[c], where, c_send.at[c], c_recv.at[c], sib, None)
        pltpu.make_async_copy(c_buf.at[c], where, c_loc.at[c]).start()
        squares = full * full
        part = squares[:, 0:128]
        for j in range(1, kc // 128):
            part = part + squares[:, j * 128:(j + 1) * 128]
        sq[...] = part if c == 0 else sq[...] + part

    for c in range(chunks):
        crossings(lp + last + c)
        relays(lp + last + c + 1)
        own_proj[c].wait()
        others(lp + c)
        x_out[c] = project(c, rows_t).astype(jnp.bfloat16)
        begin(x_out.at[c], x_in.at[c], xs_sem.at[c], xr_sem.at[c], mate, None)
        acc[:, pl.ds(c * kc, kc)] = project(c, 0)
        if c > 0:
            finish(c - 1)
    finish(chunks - 1)

    total = jnp.sum(sq[...].T, axis=0, keepdims=True)
    e_buf[...] = jnp.log(total / width_k + 1e-6)
    begin(e_buf, energy.at[s], e_sem.at[0], e_sem.at[1], sib, None)
    e_loc = pltpu.make_async_copy(e_buf, energy.at[s], e_sem.at[2])
    e_loc.start()
    e_loc.wait()
    for c in range(chunks):
        cols = pl.ds(c * kc, kc)
        mine = out.at[pl.ds(s * rows_t, rows_t), cols]
        pltpu.make_async_copy(c_buf.at[c], mine, c_loc.at[c]).wait()
        theirs = out.at[pl.ds((1 - s) * rows_t, rows_t), cols]
        rc(c_buf.at[c], theirs, c_send.at[c], c_recv.at[c], sib).wait_recv()
    rc(e_buf, energy.at[1 - s], e_sem.at[0], e_sem.at[1], sib).wait_recv()
    for src, dst, ss, rs, dev, cond in sent:
        guard(cond, lambda: rc(src, dst, ss, rs, dev).wait_send())


def write_out(coords, energy, coords_out, energy_out, sem):
    n = sem.shape[0]
    rows = coords.shape[0] // n
    half = energy.shape[2]
    copies = []
    for i in range(n):
        part = pl.ds(i * rows, rows)
        copies.append(pltpu.make_async_copy(coords.at[part, :], coords_out.at[part, :], sem.at[i]))
        copies[-1].start()
    for i in range(2):
        energy_out[pl.ds(i * half, half)] = energy[i, 0, :]
    for copy in copies:
        copy.wait()


def solution(mesh):
    nb = mesh.shape["blk"]
    ny = 2 if nb % 2 == 0 and nb <= 8 else 1

    def per_device(tiles, landmarks, projection, offsets):
        rows, width = tiles.shape
        hr, rows_t = landmarks.shape[0] // 2, rows // 2
        width_k = projection.shape[1]
        chunks = 4
        kc = width_k // chunks
        lp = 2 if hr % 32 == 0 and nb <= 8 else 1
        off = offsets.reshape(2, 1, hr)
        group = 2 if nb % 2 == 0 else 1
        bf, f32 = jnp.bfloat16, jnp.float32
        dma = pltpu.SemaphoreType.DMA
        coords, energy = pl.pallas_call(
            functools.partial(kernel, nb, ny, chunks),
            out_shape=(
                jax.ShapeDtypeStruct((rows, width_k), bf),
                jax.ShapeDtypeStruct((2, 1, rows_t), f32),
            ),
            in_specs=[pl.BlockSpec(memory_space=pl.ANY)] * 4,
            out_specs=[pl.BlockSpec(memory_space=pl.ANY)] * 2,
            scratch_shapes=[
                pltpu.VMEM((rows, width), bf),
                pltpu.VMEM((nb, 2, hr, width), bf),
                pltpu.VMEM((nb, 2, 1, hr), f32),
                pltpu.VMEM((chunks, nb, 2, hr, kc), bf),
                pltpu.VMEM((nb // group, rows, group * 2 * hr), bf),
                pltpu.VMEM((rows_t, width_k), f32),
                pltpu.VMEM((chunks, rows_t, kc), bf),
                pltpu.VMEM((chunks, rows_t, kc), bf),
                pltpu.VMEM((chunks, rows_t, kc), bf),
                pltpu.VMEM((1, rows_t), f32),
                pltpu.VMEM((rows_t, 128), f32),
                dma((lp, nb, 2)), dma((nb, 2)), dma((chunks, nb, 2)),
                dma((lp, 4, nb)), dma((4, nb)), dma((chunks, 4, nb)),
                dma((3 + chunks,)), dma, dma, dma((chunks,)), dma((chunks,)),
                dma((chunks,)), dma((chunks,)), dma((chunks,)), dma((3,)),
            ],
            compiler_params=pltpu.CompilerParams(
                collective_id=0, has_side_effects=True, vmem_limit_bytes=56 * 2**20
            ),
        )(tiles, landmarks, projection, off)
        return pl.pallas_call(
            write_out,
            out_shape=(
                jax.ShapeDtypeStruct((rows, width_k), bf),
                jax.ShapeDtypeStruct((rows,), f32),
            ),
            in_specs=[pl.BlockSpec(memory_space=pl.ANY), pl.BlockSpec(memory_space=pltpu.VMEM)],
            out_specs=(pl.BlockSpec(memory_space=pl.ANY), pl.BlockSpec(memory_space=pltpu.VMEM)),
            scratch_shapes=[dma((8,))],
        )(coords, energy)

    return jax.shard_map(
        per_device,
        mesh=mesh,
        in_specs=(
            P(("groups", "blk"), None),
            P(("blk", "split"), None),
            P(("blk", "split"), None),
            P(("blk", "split")),
        ),
        out_specs=(P(("groups", "blk"), None), P(("groups", "blk"))),
        check_vma=False,
    )
```

```python
import functools

import jax
import jax.numpy as jnp
from jax import lax
from jax.experimental import pallas as pl
from jax.experimental.pallas import tpu as pltpu
from jax.sharding import PartitionSpec as P

MESH = pl.DeviceIdType.MESH
UP, DOWN, ACROSS, SIB = 0, 1, 2, 3


def kernel(
    nb, ny, chunks,
    tiles, land, proj, off, out, energy,
    t_buf, l_buf, o_buf, p_buf, k_buf, acc, x_out, x_in, c_buf, e_buf, sq,
    r_land, r_off, r_proj, s_land, s_off, s_proj,
    loc_sem, t_send, t_recv, xs_sem, xr_sem, c_send, c_recv, c_loc, e_sem,
):
    nz = nb // ny
    g, me, s = lax.axis_index("groups"), lax.axis_index("blk"), lax.axis_index("split")
    half = lax.rem(g, 2)
    z, y = me // ny, lax.rem(me, ny)
    rows_t = t_buf.shape[0] // 2
    hr = l_buf.shape[2]
    width_k = acc.shape[1]
    kc = width_k // chunks
    lp = r_land.shape[0]
    pr = hr // lp
    J = lp + chunks
    lead = 2
    turned = (lp,) if ny == 2 else ()
    scale = 1.0 / l_buf.shape[3] ** 0.5

    mate = {"groups": g + 1 - 2 * half}
    sib = {"split": 1 - s}
    peers = {
        UP: ({"blk": me + ny}, z + 1 < nz),
        DOWN: ({"blk": me - ny}, z > 0),
        ACROSS: ({"blk": me + 1 - 2 * y}, None),
        SIB: (sib, None),
    }
    dirs = [UP, DOWN, SIB] + ([ACROSS] if ny == 2 else [])

    def guard(cond, fn):
        if cond is None:
            fn()
        else:
            pl.when(cond)(fn)

    barrier = pltpu.get_barrier_semaphore()

    def greet(dev):
        pl.semaphore_signal(barrier, inc=1, device_id=dev, device_id_type=MESH)

    greet(mate)
    for d in dirs:
        guard(peers[d][1], functools.partial(greet, peers[d][0]))
    pl.semaphore_wait(
        barrier,
        len(dirs) - 1 + (z + 1 < nz).astype(jnp.int32) + (z > 0).astype(jnp.int32),
    )

    def rc(src, dst, ss, rs, dev):
        return pltpu.make_async_remote_copy(
            src_ref=src, dst_ref=dst, send_sem=ss, recv_sem=rs, device_id=dev, device_id_type=MESH
        )

    sent = []

    def begin(src, dst, ss, rs, dev, cond):
        guard(cond, lambda: rc(src, dst, ss, rs, dev).start())
        sent.append((src, dst, ss, rs, dev, cond))

    def both(a, b):
        if a is None:
            return b
        return a if b is None else jnp.logical_and(a, b)

    def pieces(j, b, t):
        if j >= lp:
            c = j - lp
            return [(p_buf.at[c, b, t], r_proj.at[c, b, t], s_proj.at[c])]
        out = [(l_buf.at[b, t, pl.ds(j * pr, pr), :], r_land.at[j, b, t], s_land.at[j])]
        if j == 0:
            out.append((o_buf.at[b, t], r_off.at[b, t], s_off))
        return out

    def own_src(j):
        if j >= lp:
            return [proj.at[pl.ds(half * hr, hr), pl.ds((j - lp) * kc, kc)]]
        out = [land.at[pl.ds(half * hr + j * pr, pr), :]]
        if j == 0:
            out.append(off)
        return out

    def send(kind, b, d, cond=None, own=False):
        dev, exists = peers[d]
        for i, (ref, rs, ss) in enumerate(pieces(kind, b, s)):
            src = own_src(kind)[i] if own else ref
            begin(src, ref, ss.at[d, b], rs, dev, both(cond, exists))

    def await_piece(kind, b, t, cond=None):
        def go():
            for ref, rs, ss in pieces(kind, b, t):
                rc(ref, ref, rs, rs, sib).wait_recv()
        guard(cond, go)

    def send_own(kind):
        for d in dirs:
            send(kind, me, d, own=True)

    def across_of(b):
        return b + 1 - 2 * lax.rem(b, 2)

    def cands(k):
        return [(me - ny * k, z - k >= 0, UP), (me + ny * k, z + k < nz, DOWN)]

    def relay(j, k):
        for b, cond, d in cands(k):
            b = jnp.where(cond, b, me)
            await_piece(j, b, s, cond)
            send(j, b, d, cond)
            if ny == 2 and j not in turned:
                send(j, b, ACROSS, cond)
            send(j, b, SIB, cond)

    def arrive_across(j, k):
        for b, cond, d in ([(me, None, None)] if k == 0 else cands(k)):
            if d is not None:
                b = jnp.where(cond, b, me)
            b = across_of(b)
            await_piece(j, b, s, cond)
            if j in turned:
                for way in ([UP, DOWN] if d is None else [d]):
                    send(j, b, way, cond)
            send(j, b, SIB, cond)

    def relays(t):
        if t < J and t >= lead:
            send_own(t)
        for k in range(1, nz):
            if 0 <= t - k < J:
                relay(t - k, k)

    def crossings(t):
        if ny == 2:
            for k in range(nz):
                if 0 <= t - 1 - k < J:
                    arrive_across(t - 1 - k, k)

    my_rows = tiles.at[pl.ds(s * rows_t, rows_t), :]
    for j in range(lead):
        send_own(j)
    begin(my_rows, t_buf.at[pl.ds(rows_t, rows_t), :], t_send, t_recv, mate, None)
    own_tiles = pltpu.make_async_copy(my_rows, t_buf.at[pl.ds(0, rows_t), :], loc_sem.at[0])
    own_tiles.start()
    own_off = pltpu.make_async_copy(off, o_buf.at[me, s], loc_sem.at[1])
    own_off.start()
    own_land = pltpu.make_async_copy(land.at[pl.ds(half * hr, hr), :], l_buf.at[me, s], loc_sem.at[2])
    own_land.start()
    own_proj = []
    for c in range(chunks):
        cp = pltpu.make_async_copy(own_src(lp + c)[0], p_buf.at[c, me, s], loc_sem.at[3 + c])
        cp.start()
        own_proj.append(cp)

    last = nz - 1 + (1 if ny == 2 else 0)
    for t in range(lp + last):
        relays(t)
        crossings(t)
    relays(lp + last)

    own_tiles.wait()
    own_off.wait()
    own_land.wait()

    def others(kind):
        def body(b, carry):
            await_piece(kind, b, 1 - s)
            return carry
        lax.fori_loop(0, nb, body, 0)

    for j in range(lp):
        others(j)
    group = 2 if nb % 2 == 0 else 1
    gw = group * 2 * hr

    def scores(row0):
        def body(i, carry):
            rhs = l_buf[pl.ds(i * group, group)].reshape(gw, l_buf.shape[3])
            sc = lax.dot_general(
                t_buf[pl.ds(row0, rows_t), :], rhs, (((1,), (1,)), ((), ())),
                preferred_element_type=jnp.float32,
            )
            ob = o_buf[pl.ds(i * group, group)]
            ob = [jnp.where(half == 0, ob[j, t][:, :hr], ob[j, t][:, hr:]) for j in range(group) for t in range(2)]
            ob = jnp.concatenate(ob, axis=1)
            k_buf[i, pl.ds(row0, rows_t), :] = jnp.exp(sc * scale - ob).astype(jnp.bfloat16)
            return carry
        lax.fori_loop(0, nb // group, body, 0)

    scores(0)
    rc(my_rows, t_buf.at[pl.ds(rows_t, rows_t), :], t_send, t_recv, mate).wait_recv()
    scores(rows_t)

    def project(c, row0):
        total = jnp.zeros((rows_t, kc), jnp.float32)
        def body(i, total):
            rhs = p_buf[c, pl.ds(i * group, group)].reshape(gw, kc)
            return total + jnp.dot(
                k_buf[i, pl.ds(row0, rows_t), :], rhs, preferred_element_type=jnp.float32
            )
        return lax.fori_loop(0, nb // group, body, total, unroll=nb <= 8)

    def finish(c):
        rc(x_in.at[c], x_in.at[c], xs_sem.at[c], xr_sem.at[c], mate).wait_recv()
        cols = pl.ds(c * kc, kc)
        full = acc[:, cols] + x_in[c].astype(jnp.float32)
        c_buf[c] = full.astype(jnp.bfloat16)
        where = out.at[pl.ds(s * rows_t, rows_t), cols]
        begin(c_buf.at[c], where, c_send.at[c], c_recv.at[c], sib, None)
        pltpu.make_async_copy(c_buf.at[c], where, c_loc.at[c]).start()
        squares = full * full
        part = squares[:, 0:128]
        for j in range(1, kc // 128):
            part = part + squares[:, j * 128:(j + 1) * 128]
        sq[...] = part if c == 0 else sq[...] + part

    for c in range(chunks):
        crossings(lp + last + c)
        relays(lp + last + c + 1)
        own_proj[c].wait()
        others(lp + c)
        x_out[c] = project(c, rows_t).astype(jnp.bfloat16)
        begin(x_out.at[c], x_in.at[c], xs_sem.at[c], xr_sem.at[c], mate, None)
        acc[:, pl.ds(c * kc, kc)] = project(c, 0)
        if c > 0:
            finish(c - 1)
    finish(chunks - 1)

    total = jnp.sum(sq[...].T, axis=0, keepdims=True)
    e_buf[...] = jnp.log(total / width_k + 1e-6)
    begin(e_buf, energy.at[s], e_sem.at[0], e_sem.at[1], sib, None)
    e_loc = pltpu.make_async_copy(e_buf, energy.at[s], e_sem.at[2])
    e_loc.start()
    e_loc.wait()
    for c in range(chunks):
        cols = pl.ds(c * kc, kc)
        mine = out.at[pl.ds(s * rows_t, rows_t), cols]
        pltpu.make_async_copy(c_buf.at[c], mine, c_loc.at[c]).wait()
        theirs = out.at[pl.ds((1 - s) * rows_t, rows_t), cols]
        rc(c_buf.at[c], theirs, c_send.at[c], c_recv.at[c], sib).wait_recv()
    rc(e_buf, energy.at[1 - s], e_sem.at[0], e_sem.at[1], sib).wait_recv()
    for src, dst, ss, rs, dev, cond in sent:
        guard(cond, lambda: rc(src, dst, ss, rs, dev).wait_send())


def solution(mesh):
    nb = mesh.shape["blk"]
    ny = 2 if nb % 2 == 0 and nb <= 8 else 1

    def per_device(tiles, landmarks, projection, offsets):
        rows, width = tiles.shape
        hr, rows_t = landmarks.shape[0] // 2, rows // 2
        width_k = projection.shape[1]
        chunks = 2
        kc = width_k // chunks
        lp = 2 if hr % 32 == 0 and nb <= 8 else 1
        off = offsets.reshape(1, 2 * hr)
        group = 2 if nb % 2 == 0 else 1
        bf, f32 = jnp.bfloat16, jnp.float32
        dma = pltpu.SemaphoreType.DMA
        coords, energy = pl.pallas_call(
            functools.partial(kernel, nb, ny, chunks),
            out_shape=(
                jax.ShapeDtypeStruct((rows, width_k), bf),
                jax.ShapeDtypeStruct((2, 1, rows_t), f32),
            ),
            in_specs=[pl.BlockSpec(memory_space=pl.ANY)] * 4,
            out_specs=[pl.BlockSpec(memory_space=pl.ANY)] * 2,
            scratch_shapes=[
                pltpu.VMEM((rows, width), bf),
                pltpu.VMEM((nb, 2, hr, width), bf),
                pltpu.VMEM((nb, 2, 1, 2 * hr), f32),
                pltpu.VMEM((chunks, nb, 2, hr, kc), bf),
                pltpu.VMEM((nb // group, rows, group * 2 * hr), bf),
                pltpu.VMEM((rows_t, width_k), f32),
                pltpu.VMEM((chunks, rows_t, kc), bf),
                pltpu.VMEM((chunks, rows_t, kc), bf),
                pltpu.VMEM((chunks, rows_t, kc), bf),
                pltpu.VMEM((1, rows_t), f32),
                pltpu.VMEM((rows_t, 128), f32),
                dma((lp, nb, 2)), dma((nb, 2)), dma((chunks, nb, 2)),
                dma((lp, 4, nb)), dma((4, nb)), dma((chunks, 4, nb)),
                dma((3 + chunks,)), dma, dma, dma((chunks,)), dma((chunks,)),
                dma((chunks,)), dma((chunks,)), dma((chunks,)), dma((3,)),
            ],
            compiler_params=pltpu.CompilerParams(
                collective_id=0, has_side_effects=True, vmem_limit_bytes=56 * 2**20
            ),
        )(tiles, landmarks, projection, off)
        return coords, energy.reshape(rows)

    return jax.shard_map(
        per_device,
        mesh=mesh,
        in_specs=(
            P(("groups", "blk"), None),
            P(("blk", "split"), None),
            P(("blk", "split"), None),
            P(("blk", "split")),
        ),
        out_specs=(P(("groups", "blk"), None), P(("groups", "blk"))),
        check_vma=False,
    )
```

```python
import functools

import jax
import jax.numpy as jnp
from jax import lax
from jax.experimental import pallas as pl
from jax.experimental.pallas import tpu as pltpu
from jax.sharding import PartitionSpec as P

MESH = pl.DeviceIdType.MESH
UP, DOWN, ACROSS, SIB = 0, 1, 2, 3


def kernel(
    nb, ny, chunks,
    tiles, land, proj, off, out, energy,
    t_buf, l_buf, o_buf, p_buf, k_buf, acc, x_out, x_in, c_buf, e_buf, sq,
    r_land, r_off, r_proj, s_land, s_off, s_proj,
    loc_sem, t_send, t_recv, xs_sem, xr_sem, c_send, c_recv, c_loc, e_sem,
):
    nz = nb // ny
    g, me, s = lax.axis_index("groups"), lax.axis_index("blk"), lax.axis_index("split")
    half = lax.rem(g, 2)
    z, y = me // ny, lax.rem(me, ny)
    rows_t = t_buf.shape[0] // 2
    hr = l_buf.shape[2]
    width_k = acc.shape[1]
    kc = width_k // chunks
    kw = x_in.shape[2]
    sub = kc // kw
    lp = r_land.shape[0]
    pr = hr // lp
    J = lp + chunks
    lead = 2
    turned = (lp,) if ny == 2 else ()
    scale = 1.0 / l_buf.shape[3] ** 0.5

    mate = {"groups": g + 1 - 2 * half}
    sib = {"split": 1 - s}
    peers = {
        UP: ({"blk": me + ny}, z + 1 < nz),
        DOWN: ({"blk": me - ny}, z > 0),
        ACROSS: ({"blk": me + 1 - 2 * y}, None),
        SIB: (sib, None),
    }
    dirs = [UP, DOWN, SIB] + ([ACROSS] if ny == 2 else [])

    def guard(cond, fn):
        if cond is None:
            fn()
        else:
            pl.when(cond)(fn)

    barrier = pltpu.get_barrier_semaphore()

    def greet(dev):
        pl.semaphore_signal(barrier, inc=1, device_id=dev, device_id_type=MESH)

    greet(mate)
    for d in dirs:
        guard(peers[d][1], functools.partial(greet, peers[d][0]))
    pl.semaphore_wait(
        barrier,
        len(dirs) - 1 + (z + 1 < nz).astype(jnp.int32) + (z > 0).astype(jnp.int32),
    )

    def rc(src, dst, ss, rs, dev):
        return pltpu.make_async_remote_copy(
            src_ref=src, dst_ref=dst, send_sem=ss, recv_sem=rs, device_id=dev, device_id_type=MESH
        )

    sent = []

    def begin(src, dst, ss, rs, dev, cond):
        guard(cond, lambda: rc(src, dst, ss, rs, dev).start())
        sent.append((src, dst, ss, rs, dev, cond))

    def both(a, b):
        if a is None:
            return b
        return a if b is None else jnp.logical_and(a, b)

    def pieces(j, b, t):
        if j >= lp:
            c = j - lp
            return [(p_buf.at[c, b, t], r_proj.at[c, b, t], s_proj.at[c])]
        out = [(l_buf.at[b, t, pl.ds(j * pr, pr), :], r_land.at[j, b, t], s_land.at[j])]
        if j == 0:
            out.append((o_buf.at[b, t], r_off.at[b, t], s_off))
        return out

    def own_src(j):
        if j >= lp:
            return [proj.at[pl.ds(half * hr, hr), pl.ds((j - lp) * kc, kc)]]
        out = [land.at[pl.ds(half * hr + j * pr, pr), :]]
        if j == 0:
            out.append(off)
        return out

    def send(kind, b, d, cond=None, own=False):
        dev, exists = peers[d]
        for i, (ref, rs, ss) in enumerate(pieces(kind, b, s)):
            src = own_src(kind)[i] if own else ref
            begin(src, ref, ss.at[d, b], rs, dev, both(cond, exists))

    def await_piece(kind, b, t, cond=None):
        def go():
            for ref, rs, ss in pieces(kind, b, t):
                rc(ref, ref, rs, rs, sib).wait_recv()
        guard(cond, go)

    def send_own(kind):
        for d in dirs:
            send(kind, me, d, own=True)

    def across_of(b):
        return b + 1 - 2 * lax.rem(b, 2)

    def cands(k):
        return [(me - ny * k, z - k >= 0, UP), (me + ny * k, z + k < nz, DOWN)]

    def relay(j, k):
        for b, cond, d in cands(k):
            b = jnp.where(cond, b, me)
            await_piece(j, b, s, cond)
            send(j, b, d, cond)
            if ny == 2 and j not in turned:
                send(j, b, ACROSS, cond)
            send(j, b, SIB, cond)

    def arrive_across(j, k):
        for b, cond, d in ([(me, None, None)] if k == 0 else cands(k)):
            if d is not None:
                b = jnp.where(cond, b, me)
            b = across_of(b)
            await_piece(j, b, s, cond)
            if j in turned:
                for way in ([UP, DOWN] if d is None else [d]):
                    send(j, b, way, cond)
            send(j, b, SIB, cond)

    def relays(t):
        if t < J and t >= lead:
            send_own(t)
        for k in range(1, nz):
            if 0 <= t - k < J:
                relay(t - k, k)

    def crossings(t):
        if ny == 2:
            for k in range(nz):
                if 0 <= t - 1 - k < J:
                    arrive_across(t - 1 - k, k)

    my_rows = tiles.at[pl.ds(s * rows_t, rows_t), :]
    for j in range(lead):
        send_own(j)
    begin(my_rows, t_buf.at[pl.ds(rows_t, rows_t), :], t_send, t_recv, mate, None)
    own_tiles = pltpu.make_async_copy(my_rows, t_buf.at[pl.ds(0, rows_t), :], loc_sem.at[0])
    own_tiles.start()
    own_off = pltpu.make_async_copy(off, o_buf.at[me, s], loc_sem.at[1])
    own_off.start()
    own_land = pltpu.make_async_copy(land.at[pl.ds(half * hr, hr), :], l_buf.at[me, s], loc_sem.at[2])
    own_land.start()
    own_proj = []
    for c in range(chunks):
        cp = pltpu.make_async_copy(own_src(lp + c)[0], p_buf.at[c, me, s], loc_sem.at[3 + c])
        cp.start()
        own_proj.append(cp)

    last = nz - 1 + (1 if ny == 2 else 0)
    for t in range(lp + last):
        relays(t)
        crossings(t)
    relays(lp + last)

    own_tiles.wait()
    own_off.wait()
    own_land.wait()

    def others(kind):
        def body(b, carry):
            await_piece(kind, b, 1 - s)
            return carry
        lax.fori_loop(0, nb, body, 0)

    for j in range(lp):
        others(j)
    group = 2 if nb % 2 == 0 else 1
    gw = group * 2 * hr

    def scores(row0):
        def body(i, carry):
            rhs = l_buf[pl.ds(i * group, group)].reshape(gw, l_buf.shape[3])
            sc = lax.dot_general(
                t_buf[pl.ds(row0, rows_t), :], rhs, (((1,), (1,)), ((), ())),
                preferred_element_type=jnp.float32,
            )
            ob = o_buf[pl.ds(i * group, group)]
            ob = [jnp.where(half == 0, ob[j, t][:, :hr], ob[j, t][:, hr:]) for j in range(group) for t in range(2)]
            ob = jnp.concatenate(ob, axis=1)
            k_buf[i, pl.ds(row0, rows_t), :] = jnp.exp(sc * scale - ob).astype(jnp.bfloat16)
            return carry
        lax.fori_loop(0, nb // group, body, 0)

    scores(0)
    rc(my_rows, t_buf.at[pl.ds(rows_t, rows_t), :], t_send, t_recv, mate).wait_recv()
    scores(rows_t)

    def project(c, q, row0):
        def body(i, total):
            rhs = p_buf[c, pl.ds(i * group, group), :, :, q * kw:(q + 1) * kw].reshape(gw, kw)
            return total + jnp.dot(
                k_buf[i, pl.ds(row0, rows_t), :], rhs, preferred_element_type=jnp.float32
            )
        total = jnp.zeros((rows_t, kw), jnp.float32)
        return lax.fori_loop(0, nb // group, body, total, unroll=nb <= 8)

    def finish(c):
        rc(x_in.at[c], x_in.at[c], xs_sem.at[c], xr_sem.at[c], mate).wait_recv()
        cols = pl.ds(c * kw, kw)
        full = acc[:, cols] + x_in[c].astype(jnp.float32)
        c_buf[c] = full.astype(jnp.bfloat16)
        where = out.at[pl.ds(s * rows_t, rows_t), cols]
        begin(c_buf.at[c], where, c_send.at[c], c_recv.at[c], sib, None)
        pltpu.make_async_copy(c_buf.at[c], where, c_loc.at[c]).start()
        squares = full * full
        part = squares[:, 0:128]
        for j in range(1, kw // 128):
            part = part + squares[:, j * 128:(j + 1) * 128]
        sq[...] = part if c == 0 else sq[...] + part

    for c in range(chunks):
        crossings(lp + last + c)
        relays(lp + last + c + 1)
        own_proj[c].wait()
        others(lp + c)
        for q in range(sub):
            i = c * sub + q
            x_out[i] = project(c, q, rows_t).astype(jnp.bfloat16)
            begin(x_out.at[i], x_in.at[i], xs_sem.at[i], xr_sem.at[i], mate, None)
        for q in range(sub):
            acc[:, pl.ds(c * kc + q * kw, kw)] = project(c, q, 0)
        if c > 0:
            for q in range(sub):
                finish((c - 1) * sub + q)
    for q in range(sub):
        finish((chunks - 1) * sub + q)

    total = jnp.sum(sq[...].T, axis=0, keepdims=True)
    e_buf[...] = jnp.log(total / width_k + 1e-6)
    begin(e_buf, energy.at[s], e_sem.at[0], e_sem.at[1], sib, None)
    e_loc = pltpu.make_async_copy(e_buf, energy.at[s], e_sem.at[2])
    e_loc.start()
    e_loc.wait()
    for c in range(chunks * sub):
        cols = pl.ds(c * kw, kw)
        mine = out.at[pl.ds(s * rows_t, rows_t), cols]
        pltpu.make_async_copy(c_buf.at[c], mine, c_loc.at[c]).wait()
        theirs = out.at[pl.ds((1 - s) * rows_t, rows_t), cols]
        rc(c_buf.at[c], theirs, c_send.at[c], c_recv.at[c], sib).wait_recv()
    rc(e_buf, energy.at[1 - s], e_sem.at[0], e_sem.at[1], sib).wait_recv()
    for src, dst, ss, rs, dev, cond in sent:
        guard(cond, lambda: rc(src, dst, ss, rs, dev).wait_send())


def solution(mesh):
    nb = mesh.shape["blk"]
    ny = 2 if nb % 2 == 0 and nb <= 8 else 1

    def per_device(tiles, landmarks, projection, offsets):
        rows, width = tiles.shape
        hr, rows_t = landmarks.shape[0] // 2, rows // 2
        width_k = projection.shape[1]
        chunks, sub = 2, 2
        kc = width_k // chunks
        lp = 2 if hr % 32 == 0 and nb <= 8 else 1
        off = offsets.reshape(1, 2 * hr)
        group = 2 if nb % 2 == 0 else 1
        bf, f32 = jnp.bfloat16, jnp.float32
        dma = pltpu.SemaphoreType.DMA
        coords, energy = pl.pallas_call(
            functools.partial(kernel, nb, ny, chunks),
            out_shape=(
                jax.ShapeDtypeStruct((rows, width_k), bf),
                jax.ShapeDtypeStruct((2, 1, rows_t), f32),
            ),
            in_specs=[pl.BlockSpec(memory_space=pl.ANY)] * 4,
            out_specs=[pl.BlockSpec(memory_space=pl.ANY)] * 2,
            scratch_shapes=[
                pltpu.VMEM((rows, width), bf),
                pltpu.VMEM((nb, 2, hr, width), bf),
                pltpu.VMEM((nb, 2, 1, 2 * hr), f32),
                pltpu.VMEM((chunks, nb, 2, hr, kc), bf),
                pltpu.VMEM((nb // group, rows, group * 2 * hr), bf),
                pltpu.VMEM((rows_t, width_k), f32),
                pltpu.VMEM((chunks * sub, rows_t, kc // sub), bf),
                pltpu.VMEM((chunks * sub, rows_t, kc // sub), bf),
                pltpu.VMEM((chunks * sub, rows_t, kc // sub), bf),
                pltpu.VMEM((1, rows_t), f32),
                pltpu.VMEM((rows_t, 128), f32),
                dma((lp, nb, 2)), dma((nb, 2)), dma((chunks, nb, 2)),
                dma((lp, 4, nb)), dma((4, nb)), dma((chunks, 4, nb)),
                dma((3 + chunks,)), dma, dma, dma((chunks * sub,)), dma((chunks * sub,)),
                dma((chunks * sub,)), dma((chunks * sub,)), dma((chunks * sub,)), dma((3,)),
            ],
            compiler_params=pltpu.CompilerParams(
                collective_id=0, has_side_effects=True, vmem_limit_bytes=56 * 2**20
            ),
        )(tiles, landmarks, projection, off)
        return coords, energy.reshape(rows)

    return jax.shard_map(
        per_device,
        mesh=mesh,
        in_specs=(
            P(("groups", "blk"), None),
            P(("blk", "split"), None),
            P(("blk", "split"), None),
            P(("blk", "split")),
        ),
        out_specs=(P(("groups", "blk"), None), P(("groups", "blk"))),
        check_vma=False,
    )
```
